32 devices in a mesh: row: 4 (over y, core), col: 8 (over z, x).
Axes of the slice: x: 2, y: 2, z: 4, core: 2. Of those that a mesh axis runs over, the one named last changes fastest.
Arguments:
- pan_left: bfloat16 [16, 2048, 512], P('row', 'col'), may hold values from -6 to 6
- pan_right: bfloat16 [16, 2048, 512], P('row', 'col'), may hold values from -0.125 to 0.125
- inverse: bfloat16 [2048, 2048], P('col'), may hold values from -0.25 to 1.25, as said below
- rank_list: int32 [16], replicated, may hold values from 32 to 512, as said below
Outputs:
- update_right: bfloat16 [16, 16, 2048, 512], P('row', 'col')
- update_gram: bfloat16 [16, 16, 512, 512], P('row', 'col')
The draws below stay inside these ranges and needn't reach their ends.
Inputs may be any that keep to these rules, and one draw needn't show every extreme that they name: `inverse`: lower triangular; diagonal entries lie from 0.75 to 1.25. `rank_list`: columns of a tile's factors at or beyond its rank do not count.
All inputs are finite; a program needn't handle non-finite values.
Results may differ from the reference program's by a relative error of at most 0.0065.
Values may be sent and summed in bfloat16 or wider, within the bound.
No kernel may reach another device: no remote copies, remote signals or barrier semaphores. Data moves between devices by JAX's collectives and lax.ppermute only.
A program may use at most 128 MiB of HBM per device.

```python
import math
import jax
import jax.numpy as jnp
from jax import lax

NB = 2048
RMAX = 512
NP = 16


def draw_inverse(key, part):
    base = jax.random.fold_in(key, 17)
    first, second = jax.random.split(base)
    spread = jnp.clip(jax.random.normal(first, (NB, NB), jnp.float32), -4.0, 4.0)
    lower = jnp.tril(spread * (0.5 / math.sqrt(NB)), -1)
    diag_part = 0.75 + 0.5 * jax.random.uniform(second, (NB,), jnp.float32)
    return (lower + jnp.diag(diag_part)).astype(jnp.bfloat16)


def draw_rank_list(key, part):
    base = jax.random.fold_in(key, 29)
    first, second, third = jax.random.split(base, 3)
    lowest = RMAX // 16
    values = jax.random.randint(first, (NP,), lowest, RMAX + 1, dtype=jnp.int32)
    high_spot = jax.random.randint(second, (), 0, NP, dtype=jnp.int32)
    offset = jax.random.randint(third, (), 1, NP, dtype=jnp.int32)
    low_spot = (high_spot + offset) % NP
    values = values.at[high_spot].set(RMAX).at[low_spot].set(lowest)
    return values


def block_scale(rng, shape, cuts, smallest, high):
    loudness = 1.0
    for position, blocks in cuts:
        steps = jax.random.uniform(jax.random.fold_in(jax.random.fold_in(rng, 6), position), (blocks,), jnp.float32, smallest / len(cuts), high / len(cuts))
        loudness = loudness * jnp.repeat(jnp.exp(steps), shape[position] // blocks).reshape((-1,) + (1,) * (len(shape) - 1 - position))
    return loudness


def noise(stream_key, dims, width, most, cuts=(), kind=jnp.bfloat16):
    drawn = jax.random.normal(stream_key, dims, jnp.float32) * width
    if len(cuts) > 0:
        drawn = block_scale(stream_key, dims, cuts, -0.22, 0.18) * drawn
    return jnp.clip(drawn, min=-most, max=most).astype(kind)


def setup_inputs(seed: int = 0) -> dict:
    seeds = jax.random.split(jax.random.key(seed), 5)
    pan_left = noise(seeds[0], (NP, NB, RMAX), 1.0, 6.0, ((0, 4), (1, 8)))
    pan_right = noise(seeds[1], (NP, NB, RMAX), NB ** -0.5, 0.125, ((0, 4), (1, 8)))
    inverse = draw_inverse(jax.random.fold_in(seeds[4], 71), 0)
    rank_list = draw_rank_list(jax.random.fold_in(seeds[4], 71), 0)
    return dict(pan_left=pan_left, pan_right=pan_right, inverse=inverse, rank_list=rank_list)


def solve_tile(factor, inverse):
    return jnp.dot(inverse, factor, preferred_element_type=jnp.float32).astype(jnp.bfloat16)


def reference(pan_left, pan_right, inverse, rank_list):
    solved = lax.map(lambda factor: solve_tile(factor, inverse), pan_right)
    live = (jnp.arange(RMAX, dtype=jnp.int32)[None, :] < rank_list[:, None]).astype(jnp.float32)
    indices = jnp.arange(NP, dtype=jnp.int32)

    def one_pair(first, second):
        core = lax.dot_general(solved[first], solved[second], (((0,), (0,)), ((), ())), preferred_element_type=jnp.float32)
        core = (core * live[first][:, None] * live[second][None, :]).astype(jnp.bfloat16)
        update = lax.dot_general(pan_left[second], core, (((1,), (1,)), ((), ())), preferred_element_type=jnp.float32).astype(jnp.bfloat16)
        gram = (lax.dot_general(update, update, (((0,), (0,)), ((), ())), preferred_element_type=jnp.float32) / NB).astype(jnp.bfloat16)
        return update, gram

    def one_row(first):
        return lax.map(lambda second: one_pair(first, second), indices)

    update, gram = lax.map(one_row, indices)
    return update, gram
```

```python
import functools

import jax
import jax.numpy as jnp
from jax import lax
from jax.experimental import pallas as pl
from jax.experimental.pallas import tpu as pltpu
from jax.sharding import PartitionSpec as P

NT = (((1,), (1,)), ((), ()))
NN = (((1,), (0,)), ((), ()))
BLOCK = 256
MIB = 1 << 20


def dot(a, b, dims):
    return lax.dot_general(a, b, dims, preferred_element_type=jnp.float32)


def ring_of(count):
    return list(range(0, count, 2)) + list(range(count - 1, 0, -2))


def ring_place(col, count):
    return jnp.where(col % 2 == 0, col // 2, count // 2 + (count - 1 - col) // 2)


def ring_col(place, count):
    place = place % count
    return jnp.where(place < count // 2, 2 * place, count - 1 - 2 * (place - count // 2))


def gather_row(piece, rows):
    held = [piece]
    for step in range(1, rows // 2):
        held.append(lax.ppermute(piece, "row", [(i, (i + 2 * step) % rows) for i in range(rows)]))
    swapped = [lax.ppermute(h, "row", [(i, i ^ 1) for i in range(rows)]) for h in held]
    return held + swapped


def row_ids(my_row, rows):
    other = jnp.bitwise_xor(my_row, 1)
    half = rows // 2
    return [(my_row - 2 * k) % rows for k in range(half)] + [(other - 2 * k) % rows for k in range(half)]


def solve_kernel(cols, rows, meta, *refs):
    it = iter(refs)
    cw = [next(it) for _ in range(cols)]
    ccw = [next(it) for _ in range(cols)]
    sent = [[next(it) for _ in range(cols)] for _ in range(3)]
    inv = [next(it) for _ in range(rows)]
    out, right, whole, solved, rsem, isem = it
    kind, core = meta[0], meta[1]
    width = right.shape[1] // cols
    pulls = []
    for s in range(cols):
        spot = pl.multiple_of(meta[2 + s] * width, width)
        target = right.at[:, pl.ds(spot, width)]
        for case in range(5):
            ref = (cw[s].at[core], ccw[s].at[core], sent[0][s], sent[1][s], sent[2][s])[case]

            @pl.when(kind == case)
            def _(ref=ref, target=target, s=s):
                pltpu.make_async_copy(ref, target, rsem.at[s]).start()

        pulls.append(pltpu.make_async_copy(sent[0][s], target, rsem.at[s]))
    for k in range(rows):
        copy = pltpu.make_async_copy(inv[k], whole.at[:, meta[2 + cols + k]], isem.at[k])
        copy.start()
        pulls.append(copy)
    for copy in pulls:
        copy.wait()
    size = right.shape[1]
    flat = whole.reshape(size, size)
    for b in range(size // BLOCK):
        end = (b + 1) * BLOCK
        solved[:, b * BLOCK : end] = dot(right[:, :end], flat[b * BLOCK : end, :end], NT).astype(jnp.bfloat16)
    for b in range(size // BLOCK):
        start = b * BLOCK
        out[:, start : start + BLOCK] = dot(
            solved[:, start:], flat[start:, start : start + BLOCK], NN
        ).astype(jnp.bfloat16)


def main_kernel(cols, rows, tiles, per, meta, *refs):
    it = iter(refs)
    cw = [next(it) for _ in range(cols)]
    ccw = [next(it) for _ in range(cols)]
    mine, other = next(it), next(it)
    left = [next(it) for _ in range(rows)]
    high, low = next(it), next(it)
    update, gram = next(it), next(it)
    right, turned, whole, upd, grm, sem, osem = it
    half = tiles // 2
    size, width = right.shape[2], right.shape[2] // cols
    core = meta[1]
    pulls = []

    def pull(src, dst):
        copy = pltpu.make_async_copy(src, dst, sem.at[len(pulls)])
        copy.start()
        pulls.append(copy)

    pull(mine, turned.at[core])
    pull(other, turned.at[1 - core])
    for s in range(cols):
        for part, msgs, base in ((0, cw, 2), (1, ccw, 2 + cols)):
            spot = pl.multiple_of(meta[base + s] * width, width)
            pull(msgs[s], right.at[pl.ds(part * half, half), :, pl.ds(spot, width)])
    for k in range(rows):
        pull(left[k], whole.at[:, :, meta[2 + 2 * cols + k]])
    for copy in pulls:
        copy.wait()
    base = 2 + 2 * cols + rows
    rank = right.shape[1]
    flat = whole.reshape(per, size, rank)
    chunk = min(512, size)
    row_at = lax.broadcasted_iota(jnp.int32, (rank, rank), 0)
    col_at = lax.broadcasted_iota(jnp.int32, (rank, rank), 1)

    def outs(i, j, slot):
        return (
            pltpu.make_async_copy(upd.at[slot], update.at[i, j], osem.at[0, slot]),
            pltpu.make_async_copy(grm.at[slot], gram.at[i, j], osem.at[1, slot]),
        )

    def pair(at, carry):
        i, j, slot = at // per, at % per, at % 2
        value = dot(right[i], turned[j], NT)
        live = (row_at < meta[base + i]) & (col_at < meta[base + tiles + j])
        value = jnp.where(live, value, 0.0).astype(jnp.bfloat16)

        @pl.when(at >= 2)
        def _():
            for copy in outs(i, j, slot):
                copy.wait()

        def rows_of(n, carry):
            spot = pl.multiple_of(n * chunk, chunk)
            upd[slot, pl.ds(spot, chunk), :] = dot(flat[j, pl.ds(spot, chunk), :], value, NT).astype(jnp.bfloat16)
            return carry

        lax.fori_loop(0, size // chunk, rows_of, 0)
        part = (dot(value, high[j], NN) + dot(value, low[j], NN)).astype(jnp.bfloat16)
        grm[slot] = (dot(part, value, NT) / size).astype(jnp.bfloat16)
        for copy in outs(i, j, slot):
            copy.start()
        return carry

    total = tiles * per
    lax.fori_loop(0, total, pair, 0)
    for at in range(max(0, total - 2), total):
        for copy in outs(at // per, at % per, at % 2):
            copy.wait()


def local(pan_left, pan_right, inverse, rank_list):
    tiles, slab, rank = pan_right.shape
    size = inverse.shape[1]
    rows, cols = lax.axis_size("row"), lax.axis_size("col")
    per = tiles * rows // cols
    my_row, my_col = lax.axis_index("row"), lax.axis_index("col")
    piece = slab // rows
    half = tiles // 2
    cut = pan_left.reshape(tiles, rows, piece, rank)
    cut = lax.all_to_all(cut, "row", 1, 0, tiled=False).reshape(cols, per, piece, rank)
    cut = lax.all_to_all(cut, "col", 0, 0, tiled=True)
    cut = jnp.swapaxes(cut, 0, 1)
    left = gather_row(cut, rows)
    quarter = lax.dynamic_slice_in_dim(inverse, my_row * piece, piece, 0)
    quarter = lax.all_gather(quarter, "col", axis=0, tiled=False)
    inv = gather_row(quarter, rows)
    turned = jnp.swapaxes(pan_right, 1, 2)
    ring = ring_of(cols)
    ahead = [(ring[i], ring[(i + 1) % cols]) for i in range(cols)]
    back = [(b, a) for a, b in ahead]
    cw, ccw = [turned[:half]], [turned[half:]]
    for _ in range(cols - 1):
        cw.append(lax.ppermute(cw[-1], "col", ahead))
        ccw.append(lax.ppermute(ccw[-1], "col", back))
    first_half = (my_col * per) % tiles == 0
    root = (my_col * per) // tiles
    sources = [(c * per) // tiles for c in range(cols)]
    to_partner = [(src * cols + c, (src ^ 1) * cols + c) for c, src in enumerate(sources)]

    def to_core(array, core):
        moved = None
        for step in range(1, rows // 2):
            pairs = [(src * cols + c, ((src - src % 2 + 2 * step) % rows + core) * cols + c) for c, src in enumerate(sources)]
            got = lax.ppermute(array, ("row", "col"), pairs)
            moved = got if moved is None else moved + got
        return moved

    sent = [[], [], []]
    for s in range(cols):
        give = jnp.where(first_half, cw[s], ccw[s])
        keep = lax.dynamic_index_in_dim(give, 1 - root % 2, 0, keepdims=False)
        sent[0].append(lax.ppermute(keep, ("row", "col"), to_partner))
        for core in range(2):
            sent[1 + core].append(to_core(give[core], core))
    place = ring_place(my_col, cols)
    cw_from = [ring_col(place - s + cols, cols) for s in range(cols)]
    ccw_from = [ring_col(place + s, cols) for s in range(cols)]
    ids = row_ids(my_row, rows)
    core = my_row % 2
    kind = jnp.where(
        my_row == root,
        jnp.where(first_half, 0, 1),
        jnp.where(my_row // 2 == root // 2, 2, 3 + core),
    )
    came = [jnp.where(first_half, a, b) for a, b in zip(cw_from, ccw_from)]
    meta = jnp.stack([kind, core] + came + ids).astype(jnp.int32)
    anywhere = pl.BlockSpec(memory_space=pl.ANY)
    vmem = pl.BlockSpec(memory_space=pltpu.VMEM)
    smem = pl.BlockSpec(memory_space=pltpu.SMEM)
    operands = cw + ccw + sent[0] + sent[1] + sent[2] + inv
    mine = pl.pallas_call(
        functools.partial(solve_kernel, cols, rows),
        out_shape=jax.ShapeDtypeStruct((rank, size), jnp.bfloat16),
        in_specs=[smem] + [anywhere] * len(operands),
        out_specs=vmem,
        scratch_shapes=[
            pltpu.VMEM((rank, size), jnp.bfloat16),
            pltpu.VMEM((cols, rows, piece, size), jnp.bfloat16),
            pltpu.VMEM((rank, size), jnp.bfloat16),
            pltpu.SemaphoreType.DMA((cols,)),
            pltpu.SemaphoreType.DMA((rows,)),
        ],
        compiler_params=pltpu.CompilerParams(vmem_limit_bytes=32 * MIB),
        cost_estimate=pl.CostEstimate(flops=2 * rank * size * size, bytes_accessed=2 * size * (size + 2 * rank), transcendentals=0),
        name="solve",
    )(meta, *operands)
    other = lax.ppermute(mine, "row", [(i, i ^ 1) for i in range(rows)])
    exact = sum(jnp.einsum("jcnk,jcnl->jkl", p, p, preferred_element_type=jnp.float32) for p in left)
    high = exact.astype(jnp.bfloat16)
    low = (exact - high.astype(jnp.float32)).astype(jnp.bfloat16)
    my_ranks = lax.dynamic_slice_in_dim(rank_list, my_row * tiles, tiles, 0)
    their_ranks = lax.dynamic_slice_in_dim(rank_list, my_col * per, per, 0)
    meta = jnp.concatenate([jnp.stack([kind, core] + cw_from + ccw_from + ids).astype(jnp.int32), my_ranks, their_ranks])
    operands = cw + ccw + [mine, other] + left
    pulls = 2 * cols + 2 + rows
    update, gram = pl.pallas_call(
        functools.partial(main_kernel, cols, rows, tiles, per),
        out_shape=(
            jax.ShapeDtypeStruct((tiles, per, size, rank), jnp.bfloat16),
            jax.ShapeDtypeStruct((tiles, per, rank, rank), jnp.bfloat16),
        ),
        in_specs=[smem] + [anywhere] * len(operands) + [vmem, vmem],
        out_specs=(anywhere, anywhere),
        scratch_shapes=[
            pltpu.VMEM((tiles, rank, size), jnp.bfloat16),
            pltpu.VMEM((per, rank, size), jnp.bfloat16),
            pltpu.VMEM((per, cols, rows, piece, rank), jnp.bfloat16),
            pltpu.VMEM((2, size, rank), jnp.bfloat16),
            pltpu.VMEM((2, rank, rank), jnp.bfloat16),
            pltpu.SemaphoreType.DMA((pulls,)),
            pltpu.SemaphoreType.DMA((2, 2)),
        ],
        compiler_params=pltpu.CompilerParams(vmem_limit_bytes=44 * MIB),
        cost_estimate=pl.CostEstimate(
            flops=tiles * per * (4 * rank * rank * size + 6 * rank**3),
            bytes_accessed=2 * tiles * per * size * rank + 2 * size * rank * (tiles + 2 * per),
            transcendentals=0,
        ),
        name="main",
    )(meta, *operands, high, low)
    return update, gram


def solution(mesh):
    in_specs = (P("row", "col", None), P("row", "col", None), P("col", None), P())
    out_specs = (P("row", "col", None, None), P("row", "col", None, None))
    return jax.shard_map(local, mesh=mesh, in_specs=in_specs, out_specs=out_specs, check_vma=False)
```

```python
import functools

import jax
import jax.numpy as jnp
from jax import lax
from jax.experimental import pallas as pl
from jax.experimental.pallas import tpu as pltpu
from jax.sharding import PartitionSpec as P

NT = (((1,), (1,)), ((), ()))
NN = (((1,), (0,)), ((), ()))
TN = (((0,), (0,)), ((), ()))
BLOCK = 256
MIB = 1 << 20


def dot(a, b, dims):
    return lax.dot_general(a, b, dims, preferred_element_type=jnp.float32)


def ring_of(count):
    return list(range(0, count, 2)) + list(range(count - 1, 0, -2))


def ring_place(col, count):
    return jnp.where(col % 2 == 0, col // 2, count // 2 + (count - 1 - col) // 2)


def ring_col(place, count):
    place = place % count
    return jnp.where(place < count // 2, 2 * place, count - 1 - 2 * (place - count // 2))


def tie(array, *after):
    return lax.optimization_barrier((array, *after))[0]


def gather_y(piece, rows):
    return [piece] + [
        lax.ppermute(piece, "row", [(i, (i + 2 * step) % rows) for i in range(rows)]) for step in range(1, rows // 2)
    ]


def swap_cores(held, rows):
    return [lax.ppermute(h, "row", [(i, i ^ 1) for i in range(rows)]) for h in held]


def gather_row(piece, rows):
    held = gather_y(piece, rows)
    return held + swap_cores(held, rows)


def row_ids(my_row, rows):
    other = jnp.bitwise_xor(my_row, 1)
    half = rows // 2
    return [(my_row - 2 * k) % rows for k in range(half)] + [(other - 2 * k) % rows for k in range(half)]


def solve_kernel(cols, meta, cut, *refs):
    it = iter(refs)
    inv = [next(it) for _ in range(4)]
    out, right, whole, solved, rsem, isem = it
    per, share, width = cut.shape[1:]
    core = meta[0]
    pulls = []
    for s in range(cols):
        for j in range(per):
            target = right.at[pl.ds(j * share, share), pl.ds(s * width, width)]
            pulls.append(pltpu.make_async_copy(cut.at[s, j], target, rsem.at[s, j]))
        for k in range(2):
            source = meta[1 + k * cols + s]
            pulls.append(pltpu.make_async_copy(inv[k].at[s], whole.at[source, core, k], isem.at[s, k, 0]))
            pulls.append(pltpu.make_async_copy(inv[2 + k].at[s], whole.at[source, 1 - core, k], isem.at[s, k, 1]))
    for copy in pulls:
        copy.start()
    for copy in pulls:
        copy.wait()
    size = right.shape[1]
    flat = whole.reshape(size, size)
    for b in range(size // BLOCK):
        end = (b + 1) * BLOCK
        solved[:, b * BLOCK : end] = dot(right[:, :end], flat[b * BLOCK : end, :end], NT).astype(jnp.bfloat16)
    for b in range(size // BLOCK):
        start = b * BLOCK
        out[:, start : start + BLOCK] = dot(
            solved[:, start:], flat[start:, start : start + BLOCK], NN
        ).astype(jnp.bfloat16)


def main_kernel(cols, rows, tiles, per, meta, *refs):
    it = iter(refs)
    cw = [next(it) for _ in range(cols)]
    ccw = [next(it) for _ in range(cols)]
    ours = [next(it) for _ in range(rows)]
    left = [next(it) for _ in range(rows)]
    update, gram = next(it), next(it)
    right, turned, whole, upd, grm, rsem, tsem, lsem, osem = it
    half = tiles // 2
    size, width, rank = right.shape[2], right.shape[2] // cols, right.shape[1]
    share = ours[0].shape[1]
    base = rows + 2 * cols

    def turned_copies():
        spots = [pl.multiple_of(meta[k] * share, share) for k in range(rows)]
        return [
            pltpu.make_async_copy(ours[k], turned.at[:, pl.ds(spots[k], share), :], tsem.at[k]) for k in range(rows)
        ]

    def left_copies():
        return [
            pltpu.make_async_copy(left[k].at[:, j], whole.at[j, :, meta[k]], lsem.at[k, j])
            for j in range(per)
            for k in range(rows)
        ]

    def right_copies(tile):
        msgs, start = (cw, rows) if tile < half else (ccw, rows + cols)
        spots = [pl.multiple_of(meta[start + s] * width, width) for s in range(cols)]
        return [
            pltpu.make_async_copy(
                msgs[s].at[tile % half], right.at[tile, :, pl.ds(spots[s], width)], rsem.at[tile, s]
            )
            for s in range(cols)
        ]

    for copy in turned_copies() + right_copies(0) + left_copies():
        copy.start()
    for tile in range(1, tiles):
        for copy in right_copies(tile):
            copy.start()
    for copy in turned_copies():
        copy.wait()
    flat = whole.reshape(per, size, rank)
    row_at = lax.broadcasted_iota(jnp.int32, (rank, rank), 0)
    col_at = lax.broadcasted_iota(jnp.int32, (rank, rank), 1)
    cut = rank // 2

    def outs(i, j, slot):
        return (
            pltpu.make_async_copy(upd.at[slot], update.at[i, j], osem.at[0, slot]),
            pltpu.make_async_copy(grm.at[slot], gram.at[i, j], osem.at[1, slot]),
        )

    def pair(at, carry):
        i, j, slot = at // per, at % per, at % 2
        for tile in range(tiles):

            @pl.when(at == tile * per)
            def _(tile=tile):
                for copy in right_copies(tile):
                    copy.wait()

        value = dot(right[i], turned[j], NT)
        live = (row_at < meta[base + i]) & (col_at < meta[base + tiles + j])
        value = jnp.where(live, value, 0.0).astype(jnp.bfloat16)

        @pl.when(at == 0)
        def _():
            for copy in left_copies():
                copy.wait()

        @pl.when(at >= 2)
        def _():
            for copy in outs(i, j, slot):
                copy.wait()

        upd[slot] = dot(flat[j], value, NT).astype(jnp.bfloat16)
        outs(i, j, slot)[0].start()
        top = (dot(upd[slot, :, :cut], upd[slot], TN) / size).astype(jnp.bfloat16)
        grm[slot, :cut] = top
        grm[slot, cut:, :cut] = top[:, cut:].T
        grm[slot, cut:, cut:] = (dot(upd[slot, :, cut:], upd[slot, :, cut:], TN) / size).astype(jnp.bfloat16)
        outs(i, j, slot)[1].start()
        return carry

    total = tiles * per
    lax.fori_loop(0, total, pair, 0)
    for at in range(max(0, total - 2), total):
        for copy in outs(at // per, at % per, at % 2):
            copy.wait()


def to_column(pieces):
    moved = lax.all_to_all(pieces, "row", 1, 0, tiled=False)
    cols = lax.axis_size("col")
    moved = moved.reshape((cols, -1) + pieces.shape[2:])
    return moved


def local(pan_left, pan_right, inverse, rank_list):
    tiles, slab, rank = pan_right.shape
    size = inverse.shape[1]
    rows, cols = lax.axis_size("row"), lax.axis_size("col")
    per = tiles * rows // cols
    my_row, my_col = lax.axis_index("row"), lax.axis_index("col")
    piece = slab // rows
    share = rank // rows
    half = tiles // 2
    turned = jnp.swapaxes(pan_right, 1, 2)
    place = ring_place(my_col, cols)
    cw_from = [ring_col(place - s + cols, cols) for s in range(cols)]
    ccw_from = [ring_col(place + s, cols) for s in range(cols)]
    ids = row_ids(my_row, rows)
    anywhere = pl.BlockSpec(memory_space=pltpu.HBM)
    vmem = pl.BlockSpec(memory_space=pltpu.VMEM)
    smem = pl.BlockSpec(memory_space=pltpu.SMEM)

    def solve(cut, inv):
        return pl.pallas_call(
            functools.partial(solve_kernel, cols),
            out_shape=jax.ShapeDtypeStruct((per * share, size), jnp.bfloat16),
            in_specs=[smem] + [anywhere] * 5,
            out_specs=vmem,
            scratch_shapes=[
                pltpu.VMEM((per * share, size), jnp.bfloat16),
                pltpu.VMEM((cols, 2, 2, slab // 4, size), jnp.bfloat16),
                pltpu.VMEM((per * share, size), jnp.bfloat16),
                pltpu.SemaphoreType.DMA((cols, per)),
                pltpu.SemaphoreType.DMA((cols, 2, 2)),
            ],
            compiler_params=pltpu.CompilerParams(vmem_limit_bytes=60 * MIB),
            cost_estimate=pl.CostEstimate(
                flops=2 * per * share * size * size, bytes_accessed=2 * size * (size + 2 * per * share), transcendentals=0
            ),
            name="solve",
        )(jnp.stack([my_row % 2] + cw_from + ccw_from).astype(jnp.int32), cut, *inv).reshape(per, share, size)

    cut = to_column(turned.reshape(tiles, rows, share, slab))
    ring = ring_of(cols)
    ahead = [(ring[i], ring[(i + 1) % cols]) for i in range(cols)]
    back = [(b, a) for a, b in ahead]
    part = slab // 2
    mine = lax.dynamic_slice_in_dim(inverse, (my_row % 2) * part, part, 0)
    inv_cw, inv_ccw = [mine[: part // 2]], [mine[part // 2 :]]
    for step in range(1, cols):
        inv_cw.append(lax.ppermute(inv_cw[-1], "col", ahead))
        inv_ccw.append(lax.ppermute(inv_ccw[-1], "col", back))
        held = (inv_cw[-1], inv_ccw[-1])
        if step == max(1, round((cols - 1) * 2 / 7)):
            held, cut = lax.optimization_barrier((held, cut))
            cut = lax.all_to_all(cut, "col", 0, 0, tiled=True)
        elif step == cols - 1:
            held, cut, turned = lax.optimization_barrier((held, cut, turned))
        else:
            held = lax.optimization_barrier(held)
        inv_cw[-1], inv_ccw[-1] = held
    inv = [jnp.stack(inv_cw), jnp.stack(inv_ccw)]
    inv = inv + swap_cores(inv, rows)
    cw, ccw = [turned[:half]], [turned[half:]]
    last = cols - 1
    marks = [max(1, round(last * m / 7)) for m in range(8)]
    left = pan_left
    for step in range(1, cols):
        cw.append(lax.ppermute(cw[-1], "col", ahead))
        ccw.append(lax.ppermute(ccw[-1], "col", back))
        if step == last:
            break
        held = (cw[-1], ccw[-1])
        if step == marks[1]:
            held, inv, left = lax.optimization_barrier((held, inv, left))
            ours = gather_y(solve(cut, inv), rows)
            left = to_column(left.reshape(tiles, rows, piece, rank))
        elif step == marks[2]:
            held, left = lax.optimization_barrier((held, left))
            left = lax.all_to_all(left, "col", 0, 0, tiled=True)
        elif step == marks[4]:
            held, left, ours = lax.optimization_barrier((held, left, ours))
            left = gather_y(left, rows)
            ours = ours + swap_cores(ours, rows)
        elif step == marks[6]:
            held, left, ours = lax.optimization_barrier((held, left, ours))
            left = left + swap_cores(left, rows)
        else:
            held = lax.optimization_barrier(held)
        cw[-1], ccw[-1] = held
    my_ranks = lax.dynamic_slice_in_dim(rank_list, my_row * tiles, tiles, 0)
    their_ranks = lax.dynamic_slice_in_dim(rank_list, my_col * per, per, 0)
    meta = jnp.concatenate([jnp.stack(ids + cw_from + ccw_from).astype(jnp.int32), my_ranks, their_ranks])
    operands = cw + ccw + ours + left
    update, gram = pl.pallas_call(
        functools.partial(main_kernel, cols, rows, tiles, per),
        out_shape=(
            jax.ShapeDtypeStruct((tiles, per, size, rank), jnp.bfloat16),
            jax.ShapeDtypeStruct((tiles, per, rank, rank), jnp.bfloat16),
        ),
        in_specs=[smem] + [anywhere] * len(operands),
        out_specs=(anywhere, anywhere),
        scratch_shapes=[
            pltpu.VMEM((tiles, rank, size), jnp.bfloat16),
            pltpu.VMEM((per, rank, size), jnp.bfloat16),
            pltpu.VMEM((per, cols, rows, piece, rank), jnp.bfloat16),
            pltpu.VMEM((2, size, rank), jnp.bfloat16),
            pltpu.VMEM((2, rank, rank), jnp.bfloat16),
            pltpu.SemaphoreType.DMA((tiles, cols)),
            pltpu.SemaphoreType.DMA((rows,)),
            pltpu.SemaphoreType.DMA((rows, per)),
            pltpu.SemaphoreType.DMA((2, 2)),
        ],
        compiler_params=pltpu.CompilerParams(vmem_limit_bytes=60 * MIB),
        cost_estimate=pl.CostEstimate(
            flops=tiles * per * (6 * rank * rank * size),
            bytes_accessed=2 * tiles * per * size * rank + 2 * size * rank * (tiles + 2 * per),
            transcendentals=0,
        ),
        name="main",
    )(meta, *operands)
    return update, gram


def solution(mesh):
    in_specs = (P("row", "col", None), P("row", "col", None), P("col", None), P())
    out_specs = (P("row", "col", None, None), P("row", "col", None, None))
    return jax.shard_map(local, mesh=mesh, in_specs=in_specs, out_specs=out_specs, check_vma=False)
```

```python
import functools

import jax
import jax.numpy as jnp
from jax import lax
from jax.experimental import pallas as pl
from jax.experimental.pallas import tpu as pltpu
from jax.sharding import PartitionSpec as P

NT = (((1,), (1,)), ((), ()))
NN = (((1,), (0,)), ((), ()))
TN = (((0,), (0,)), ((), ()))
BLOCK = 256
MIB = 1 << 20


def dot(a, b, dims):
    return lax.dot_general(a, b, dims, preferred_element_type=jnp.float32)


def ring_of(count):
    return list(range(0, count, 2)) + list(range(count - 1, 0, -2))


def ring_place(col, count):
    return jnp.where(col % 2 == 0, col // 2, count // 2 + (count - 1 - col) // 2)


def ring_col(place, count):
    place = place % count
    return jnp.where(place < count // 2, 2 * place, count - 1 - 2 * (place - count // 2))


def tie(array, *after):
    return lax.optimization_barrier((array, *after))[0]


def gather_y(piece, rows):
    return [piece] + [
        lax.ppermute(piece, "row", [(i, (i + 2 * step) % rows) for i in range(rows)]) for step in range(1, rows // 2)
    ]


def swap_cores(held, rows):
    return [lax.ppermute(h, "row", [(i, i ^ 1) for i in range(rows)]) for h in held]


def gather_row(piece, rows):
    held = gather_y(piece, rows)
    return held + swap_cores(held, rows)


def row_ids(my_row, rows):
    other = jnp.bitwise_xor(my_row, 1)
    half = rows // 2
    return [(my_row - 2 * k) % rows for k in range(half)] + [(other - 2 * k) % rows for k in range(half)]


def solve_kernel(cols, meta, cut, *refs):
    it = iter(refs)
    inv = [next(it) for _ in range(4)]
    per, share, width = cut.shape[1:]
    out = [next(it) for _ in range(per)]
    right, whole, solved, rsem, isem = it
    core = meta[0]
    pulls = []
    for s in range(cols):
        for j in range(per):
            target = right.at[pl.ds(j * share, share), pl.ds(s * width, width)]
            pulls.append(pltpu.make_async_copy(cut.at[s, j], target, rsem.at[s, j]))
        for k in range(2):
            source = meta[1 + k * cols + s]
            pulls.append(pltpu.make_async_copy(inv[k].at[s], whole.at[source, core, k], isem.at[s, k, 0]))
            pulls.append(pltpu.make_async_copy(inv[2 + k].at[s], whole.at[source, 1 - core, k], isem.at[s, k, 1]))
    for copy in pulls:
        copy.start()
    for copy in pulls:
        copy.wait()
    size = right.shape[1]
    flat = whole.reshape(size, size)
    for b in range(size // BLOCK):
        end = (b + 1) * BLOCK
        solved[:, b * BLOCK : end] = dot(right[:, :end], flat[b * BLOCK : end, :end], NT).astype(jnp.bfloat16)
    for b in range(size // BLOCK):
        start = b * BLOCK
        value = dot(solved[:, start:], flat[start:, start : start + BLOCK], NN).astype(jnp.bfloat16)
        for j in range(per):
            out[j][:, start : start + BLOCK] = value[j * share : (j + 1) * share]


def main_kernel(cols, rows, tiles, per, meta, *refs):
    it = iter(refs)
    cw = [next(it) for _ in range(cols)]
    ccw = [next(it) for _ in range(cols)]
    ours = [[next(it) for _ in range(rows)] for _ in range(per)]
    left = [[next(it) for _ in range(rows)] for _ in range(2)]
    update, gram = next(it), next(it)
    right, turned, whole, upd, grm, rsem, tsem, lsem, osem = it
    half = tiles // 2
    size, width, rank = right.shape[2], right.shape[2] // cols, right.shape[1]
    share, some = ours[0][0].shape[0], left[0][0].shape[0]
    base = rows + 2 * cols

    def turned_copies():
        spots = [pl.multiple_of(meta[k] * share, share) for k in range(rows)]
        return [
            pltpu.make_async_copy(ours[j][k], turned.at[j, pl.ds(spots[k], share), :], tsem.at[j, k])
            for j in range(per)
            for k in range(rows)
        ]

    def left_copies():
        return [
            pltpu.make_async_copy(
                left[h][k].at[:, j], whole.at[j, h * some : (h + 1) * some, meta[k]], lsem.at[h, k, j]
            )
            for j in range(per)
            for h in range(2)
            for k in range(rows)
        ]

    def right_copies(tile):
        msgs, start = (cw, rows) if tile < half else (ccw, rows + cols)
        spots = [pl.multiple_of(meta[start + s] * width, width) for s in range(cols)]
        return [
            pltpu.make_async_copy(
                msgs[s].at[tile % half], right.at[tile, :, pl.ds(spots[s], width)], rsem.at[tile, s]
            )
            for s in range(cols)
        ]

    for copy in turned_copies() + right_copies(0) + left_copies():
        copy.start()
    for tile in range(1, tiles):
        for copy in right_copies(tile):
            copy.start()
    for copy in turned_copies():
        copy.wait()
    flat = whole.reshape(per, size, rank)
    row_at = lax.broadcasted_iota(jnp.int32, (rank, rank), 0)
    col_at = lax.broadcasted_iota(jnp.int32, (rank, rank), 1)
    cut = rank // 2

    def outs(i, j, slot):
        return (
            pltpu.make_async_copy(upd.at[slot], update.at[i, j], osem.at[0, slot]),
            pltpu.make_async_copy(grm.at[slot], gram.at[i, j], osem.at[1, slot]),
        )

    def pair(at, carry):
        i, j, slot = at // per, at % per, at % 2
        for tile in range(tiles):

            @pl.when(at == tile * per)
            def _(tile=tile):
                for copy in right_copies(tile):
                    copy.wait()

        @pl.when(at == 0)
        def _():
            for copy in left_copies():
                copy.wait()

        @pl.when(at >= 2)
        def _():
            for copy in outs(i, j, slot):
                copy.wait()

        def work(tall, wide):
            value = dot(right[i, :tall], turned[j, :wide], NT)
            live = (row_at[:tall, :wide] < meta[base + i]) & (col_at[:tall, :wide] < meta[base + tiles + j])
            value = jnp.where(live, value, 0.0).astype(jnp.bfloat16)
            upd[slot, :, :tall] = dot(flat[j, :, :wide], value, NT).astype(jnp.bfloat16)
            if tall < rank:
                upd[slot, :, tall:] = jnp.zeros((size, rank - tall), jnp.bfloat16)
            outs(i, j, slot)[0].start()
            top = (dot(upd[slot, :, :cut], upd[slot, :, :tall], TN) / size).astype(jnp.bfloat16)
            grm[slot, :cut, :tall] = top
            if tall < rank:
                grm[slot, :cut, cut:] = jnp.zeros((cut, rank - cut), jnp.bfloat16)
                grm[slot, cut:] = jnp.zeros((rank - cut, rank), jnp.bfloat16)
            else:
                grm[slot, cut:, :cut] = top[:, cut:].T
                grm[slot, cut:, cut:] = (dot(upd[slot, :, cut:], upd[slot, :, cut:], TN) / size).astype(jnp.bfloat16)

        for tall in (cut, rank):
            for wide in (cut, rank):
                low = meta[base + i] <= cut if tall == cut else meta[base + i] > cut
                thin = meta[base + tiles + j] <= cut if wide == cut else meta[base + tiles + j] > cut

                @pl.when(jnp.logical_and(low, thin))
                def _(tall=tall, wide=wide):
                    work(tall, wide)

        outs(i, j, slot)[1].start()
        return carry

    total = tiles * per
    lax.fori_loop(0, total, pair, 0)
    for at in range(max(0, total - 2), total):
        for copy in outs(at // per, at % per, at % 2):
            copy.wait()


def to_column(pieces):
    moved = lax.all_to_all(pieces, "row", 1, 0, tiled=False)
    cols = lax.axis_size("col")
    moved = moved.reshape((cols, -1) + pieces.shape[2:])
    return moved


def local(pan_left, pan_right, inverse, rank_list):
    tiles, slab, rank = pan_right.shape
    size = inverse.shape[1]
    rows, cols = lax.axis_size("row"), lax.axis_size("col")
    per = tiles * rows // cols
    my_row, my_col = lax.axis_index("row"), lax.axis_index("col")
    piece = slab // rows
    share = rank // rows
    half = tiles // 2
    turned = jnp.swapaxes(pan_right, 1, 2)
    place = ring_place(my_col, cols)
    cw_from = [ring_col(place - s + cols, cols) for s in range(cols)]
    ccw_from = [ring_col(place + s, cols) for s in range(cols)]
    ids = row_ids(my_row, rows)
    anywhere = pl.BlockSpec(memory_space=pltpu.HBM)
    vmem = pl.BlockSpec(memory_space=pltpu.VMEM)
    smem = pl.BlockSpec(memory_space=pltpu.SMEM)

    def solve(cut, inv):
        return pl.pallas_call(
            functools.partial(solve_kernel, cols),
            out_shape=[jax.ShapeDtypeStruct((share, size), jnp.bfloat16)] * per,
            in_specs=[smem] + [anywhere] * 5,
            out_specs=[vmem] * per,
            scratch_shapes=[
                pltpu.VMEM((per * share, size), jnp.bfloat16),
                pltpu.VMEM((cols, 2, 2, slab // 4, size), jnp.bfloat16),
                pltpu.VMEM((per * share, size), jnp.bfloat16),
                pltpu.SemaphoreType.DMA((cols, per)),
                pltpu.SemaphoreType.DMA((cols, 2, 2)),
            ],
            compiler_params=pltpu.CompilerParams(vmem_limit_bytes=60 * MIB),
            cost_estimate=pl.CostEstimate(
                flops=2 * per * share * size * size, bytes_accessed=2 * size * (size + 2 * per * share), transcendentals=0
            ),
            name="solve",
        )(jnp.stack([my_row % 2] + cw_from + ccw_from).astype(jnp.int32), cut, *inv)

    cut = to_column(turned.reshape(tiles, rows, share, slab))
    ring = ring_of(cols)
    ahead = [(ring[i], ring[(i + 1) % cols]) for i in range(cols)]
    back = [(b, a) for a, b in ahead]
    part = slab // 2
    mine = lax.dynamic_slice_in_dim(inverse, (my_row % 2) * part, part, 0)
    left = pan_left
    inv_cw, inv_ccw = [mine[: part // 2]], [mine[part // 2 :]]
    for step in range(1, cols):
        inv_cw.append(lax.ppermute(inv_cw[-1], "col", ahead))
        inv_ccw.append(lax.ppermute(inv_ccw[-1], "col", back))
        held = (inv_cw[-1], inv_ccw[-1])
        if step == max(1, round((cols - 1) * 2 / 7)):
            held, cut, left = lax.optimization_barrier((held, cut, left))
            left = to_column(left.reshape(tiles, rows, piece, rank))
        elif step == max(1, round((cols - 1) * 4 / 7)):
            held, cut, left = lax.optimization_barrier((held, cut, left))
            cut = lax.all_to_all(cut, "col", 0, 0, tiled=True)
        elif step == cols - 1:
            held, turned = lax.optimization_barrier((held, turned))
        else:
            held = lax.optimization_barrier(held)
        inv_cw[-1], inv_ccw[-1] = held
    inv = [jnp.stack(inv_cw), jnp.stack(inv_ccw)]
    inv = inv + swap_cores(inv, rows)
    cw, ccw = [turned[:half]], [turned[half:]]
    last = cols - 1
    marks = [max(1, round(last * m / 7)) for m in range(8)]
    for step in range(1, cols):
        cw.append(lax.ppermute(cw[-1], "col", ahead))
        ccw.append(lax.ppermute(ccw[-1], "col", back))
        if step == last:
            break
        held = (cw[-1], ccw[-1])
        if step == marks[1]:
            held, inv, left, cut = lax.optimization_barrier((held, inv, left, cut))
            solved = solve(cut, inv)
            left = lax.all_to_all(left, "col", 0, 0, tiled=True)
        elif step == marks[2]:
            held, solved = lax.optimization_barrier((held, solved))
            first = [gather_y(part, rows) for part in solved[: per // 2]]
        elif step == marks[3]:
            held, left, first = lax.optimization_barrier((held, left, first))
            second = [gather_y(part, rows) for part in solved[per // 2 :]]
        elif step == marks[4]:
            held, second = lax.optimization_barrier((held, second))
            left = [left[: cols // 2], left[cols // 2 :]]
            left[0] = gather_y(left[0], rows)
            ours = [part + swap_cores(part, rows) for part in first]
        elif step == marks[5]:
            held, left[0], ours = lax.optimization_barrier((held, left[0], ours))
            left[1] = gather_y(left[1], rows)
            ours = ours + [part + swap_cores(part, rows) for part in second]
        elif step == marks[6]:
            held, left, ours = lax.optimization_barrier((held, left, ours))
            left = [part + swap_cores(part, rows) for part in left]
        else:
            held = lax.optimization_barrier(held)
        cw[-1], ccw[-1] = held
    my_ranks = lax.dynamic_slice_in_dim(rank_list, my_row * tiles, tiles, 0)
    their_ranks = lax.dynamic_slice_in_dim(rank_list, my_col * per, per, 0)
    meta = jnp.concatenate([jnp.stack(ids + cw_from + ccw_from).astype(jnp.int32), my_ranks, their_ranks])
    operands = cw + ccw + [a for group in ours + left for a in group]
    update, gram = pl.pallas_call(
        functools.partial(main_kernel, cols, rows, tiles, per),
        out_shape=(
            jax.ShapeDtypeStruct((tiles, per, size, rank), jnp.bfloat16),
            jax.ShapeDtypeStruct((tiles, per, rank, rank), jnp.bfloat16),
        ),
        in_specs=[smem] + [anywhere] * len(operands),
        out_specs=(anywhere, anywhere),
        scratch_shapes=[
            pltpu.VMEM((tiles, rank, size), jnp.bfloat16),
            pltpu.VMEM((per, rank, size), jnp.bfloat16),
            pltpu.VMEM((per, cols, rows, piece, rank), jnp.bfloat16),
            pltpu.VMEM((2, size, rank), jnp.bfloat16),
            pltpu.VMEM((2, rank, rank), jnp.bfloat16),
            pltpu.SemaphoreType.DMA((tiles, cols)),
            pltpu.SemaphoreType.DMA((per, rows)),
            pltpu.SemaphoreType.DMA((2, rows, per)),
            pltpu.SemaphoreType.DMA((2, 2)),
        ],
        compiler_params=pltpu.CompilerParams(vmem_limit_bytes=60 * MIB),
        cost_estimate=pl.CostEstimate(
            flops=tiles * per * (6 * rank * rank * size),
            bytes_accessed=2 * tiles * per * size * rank + 2 * size * rank * (tiles + 2 * per),
            transcendentals=0,
        ),
        name="main",
    )(meta, *operands)
    return update, gram


def solution(mesh):
    in_specs = (P("row", "col", None), P("row", "col", None), P("col", None), P())
    out_specs = (P("row", "col", None, None), P("row", "col", None, None))
    return jax.shard_map(local, mesh=mesh, in_specs=in_specs, out_specs=out_specs, check_vma=False)
```

```python
import functools

import jax
import jax.numpy as jnp
from jax import lax
from jax.experimental import pallas as pl
from jax.experimental.pallas import tpu as pltpu
from jax.sharding import PartitionSpec as P

NT = (((1,), (1,)), ((), ()))
NN = (((1,), (0,)), ((), ()))
TN = (((0,), (0,)), ((), ()))
BLOCK = 256
MIB = 1 << 20


def dot(a, b, dims):
    return lax.dot_general(a, b, dims, preferred_element_type=jnp.float32)


def ring_of(count):
    return list(range(0, count, 2)) + list(range(count - 1, 0, -2))


def ring_place(col, count):
    return jnp.where(col % 2 == 0, col // 2, count // 2 + (count - 1 - col) // 2)


def ring_col(place, count):
    place = place % count
    return jnp.where(place < count // 2, 2 * place, count - 1 - 2 * (place - count // 2))


def split_steps(cols, half):
    return (cols - 2) // half


def tie(array, *after):
    return lax.optimization_barrier((array, *after))[0]


def gather_y(piece, rows):
    return [piece] + [
        lax.ppermute(piece, "row", [(i, (i + 2 * step) % rows) for i in range(rows)]) for step in range(1, rows // 2)
    ]


def swap_cores(held, rows):
    return [lax.ppermute(h, "row", [(i, i ^ 1) for i in range(rows)]) for h in held]


def gather_row(piece, rows):
    held = gather_y(piece, rows)
    return held + swap_cores(held, rows)


def row_ids(my_row, rows):
    other = jnp.bitwise_xor(my_row, 1)
    half = rows // 2
    return [(my_row - 2 * k) % rows for k in range(half)] + [(other - 2 * k) % rows for k in range(half)]


def solve_kernel(cols, meta, cut, *refs):
    it = iter(refs)
    inv = [next(it) for _ in range(4)]
    per, share, width = cut.shape[1:]
    out = [next(it) for _ in range(per)]
    right, whole, solved, rsem, isem = it
    core = meta[0]
    pulls = []
    for s in range(cols):
        for j in range(per):
            target = right.at[pl.ds(j * share, share), pl.ds(s * width, width)]
            pulls.append(pltpu.make_async_copy(cut.at[s, j], target, rsem.at[s, j]))
        for k in range(2):
            source = meta[1 + k * cols + s]
            pulls.append(pltpu.make_async_copy(inv[k].at[s], whole.at[source, core, k], isem.at[s, k, 0]))
            pulls.append(pltpu.make_async_copy(inv[2 + k].at[s], whole.at[source, 1 - core, k], isem.at[s, k, 1]))
    for copy in pulls:
        copy.start()
    for copy in pulls:
        copy.wait()
    size = right.shape[1]
    flat = whole.reshape(size, size)
    for b in range(size // BLOCK):
        end = (b + 1) * BLOCK
        solved[:, b * BLOCK : end] = dot(right[:, :end], flat[b * BLOCK : end, :end], NT).astype(jnp.bfloat16)
    for b in range(size // BLOCK):
        start = b * BLOCK
        value = dot(solved[:, start:], flat[start:, start : start + BLOCK], NN).astype(jnp.bfloat16)
        for j in range(per):
            out[j][:, start : start + BLOCK] = value[j * share : (j + 1) * share]


def main_kernel(cols, rows, tiles, per, meta, *refs):
    it = iter(refs)
    split = split_steps(cols, tiles // 2)

    def message(step):
        if 1 <= step <= split:
            return [next(it) for _ in range(tiles // 2)]
        whole = next(it)
        return [whole.at[k] for k in range(tiles // 2)]

    cw = [message(s) for s in range(cols)]
    ccw = [message(s) for s in range(cols)]
    ours = [[next(it) for _ in range(rows)] for _ in range(per)]
    left = [[next(it) for _ in range(rows)] for _ in range(2)]
    update, gram = next(it), next(it)
    right, turned, whole, upd, grm, rsem, tsem, lsem, osem = it
    half = tiles // 2
    size, width, rank = right.shape[2], right.shape[2] // cols, right.shape[1]
    share, some = ours[0][0].shape[0], left[0][0].shape[0]
    base = rows + 2 * cols

    def turned_copies():
        spots = [pl.multiple_of(meta[k] * share, share) for k in range(rows)]
        return [
            pltpu.make_async_copy(ours[j][k], turned.at[j, pl.ds(spots[k], share), :], tsem.at[j, k])
            for j in range(per)
            for k in range(rows)
        ]

    def left_copies():
        return [
            pltpu.make_async_copy(
                left[h][k].at[:, j], whole.at[j, h * some : (h + 1) * some, meta[k]], lsem.at[h, k, j]
            )
            for j in range(per)
            for h in range(2)
            for k in range(rows)
        ]

    def right_copies(tile):
        msgs, start = (cw, rows) if tile < half else (ccw, rows + cols)
        spots = [pl.multiple_of(meta[start + s] * width, width) for s in range(cols)]
        return [
            pltpu.make_async_copy(
                msgs[s][tile % half], right.at[tile, :, pl.ds(spots[s], width)], rsem.at[tile, s]
            )
            for s in range(cols)
        ]

    for copy in turned_copies() + right_copies(0) + left_copies():
        copy.start()
    for tile in range(1, tiles):
        for copy in right_copies(tile):
            copy.start()
    for copy in turned_copies():
        copy.wait()
    flat = whole.reshape(per, size, rank)
    row_at = lax.broadcasted_iota(jnp.int32, (rank, rank), 0)
    col_at = lax.broadcasted_iota(jnp.int32, (rank, rank), 1)
    cut = rank // 2

    def outs(i, j, slot):
        return (
            pltpu.make_async_copy(upd.at[slot], update.at[i, j], osem.at[0, slot]),
            pltpu.make_async_copy(grm.at[slot], gram.at[i, j], osem.at[1, slot]),
        )

    def pair(at, carry):
        i, j, slot = at // per, at % per, at % 2
        for tile in range(tiles):

            @pl.when(at == tile * per)
            def _(tile=tile):
                for copy in right_copies(tile):
                    copy.wait()

        @pl.when(at == 0)
        def _():
            for copy in left_copies():
                copy.wait()

        @pl.when(at >= 2)
        def _():
            for copy in outs(i, j, slot):
                copy.wait()

        def work(tall, wide):
            value = dot(right[i, :tall], turned[j, :wide], NT)
            live = (row_at[:tall, :wide] < meta[base + i]) & (col_at[:tall, :wide] < meta[base + tiles + j])
            value = jnp.where(live, value, 0.0).astype(jnp.bfloat16)
            upd[slot, :, :tall] = dot(flat[j, :, :wide], value, NT).astype(jnp.bfloat16)
            if tall < rank:
                upd[slot, :, tall:] = jnp.zeros((size, rank - tall), jnp.bfloat16)
            outs(i, j, slot)[0].start()
            top = (dot(upd[slot, :, :cut], upd[slot, :, :tall], TN) / size).astype(jnp.bfloat16)
            grm[slot, :cut, :tall] = top
            if tall < rank:
                grm[slot, :cut, cut:] = jnp.zeros((cut, rank - cut), jnp.bfloat16)
                grm[slot, cut:] = jnp.zeros((rank - cut, rank), jnp.bfloat16)
            else:
                grm[slot, cut:, :cut] = top[:, cut:].T
                grm[slot, cut:, cut:] = (dot(upd[slot, :, cut:], upd[slot, :, cut:], TN) / size).astype(jnp.bfloat16)

        for tall in (cut, rank):
            for wide in (cut, rank):
                low = meta[base + i] <= cut if tall == cut else meta[base + i] > cut
                thin = meta[base + tiles + j] <= cut if wide == cut else meta[base + tiles + j] > cut

                @pl.when(jnp.logical_and(low, thin))
                def _(tall=tall, wide=wide):
                    work(tall, wide)

        outs(i, j, slot)[1].start()
        return carry

    total = tiles * per
    lax.fori_loop(0, total, pair, 0)
    for at in range(max(0, total - 2), total):
        for copy in outs(at // per, at % per, at % 2):
            copy.wait()


def to_column(pieces):
    moved = lax.all_to_all(pieces, "row", 1, 0, tiled=False)
    cols = lax.axis_size("col")
    moved = moved.reshape((cols, -1) + pieces.shape[2:])
    return moved


def local(pan_left, pan_right, inverse, rank_list):
    tiles, slab, rank = pan_right.shape
    size = inverse.shape[1]
    rows, cols = lax.axis_size("row"), lax.axis_size("col")
    per = tiles * rows // cols
    my_row, my_col = lax.axis_index("row"), lax.axis_index("col")
    piece = slab // rows
    share = rank // rows
    half = tiles // 2
    turned = jnp.swapaxes(pan_right, 1, 2)
    place = ring_place(my_col, cols)
    cw_from = [ring_col(place - s + cols, cols) for s in range(cols)]
    ccw_from = [ring_col(place + s, cols) for s in range(cols)]
    ids = row_ids(my_row, rows)
    anywhere = pl.BlockSpec(memory_space=pltpu.HBM)
    vmem = pl.BlockSpec(memory_space=pltpu.VMEM)
    smem = pl.BlockSpec(memory_space=pltpu.SMEM)

    def solve(cut, inv):
        return pl.pallas_call(
            functools.partial(solve_kernel, cols),
            out_shape=[jax.ShapeDtypeStruct((share, size), jnp.bfloat16)] * per,
            in_specs=[smem] + [anywhere] * 5,
            out_specs=[vmem] * per,
            scratch_shapes=[
                pltpu.VMEM((per * share, size), jnp.bfloat16),
                pltpu.VMEM((cols, 2, 2, slab // 4, size), jnp.bfloat16),
                pltpu.VMEM((per * share, size), jnp.bfloat16),
                pltpu.SemaphoreType.DMA((cols, per)),
                pltpu.SemaphoreType.DMA((cols, 2, 2)),
            ],
            compiler_params=pltpu.CompilerParams(vmem_limit_bytes=60 * MIB),
            cost_estimate=pl.CostEstimate(
                flops=2 * per * share * size * size, bytes_accessed=2 * size * (size + 2 * per * share), transcendentals=0
            ),
            name="solve",
        )(jnp.stack([my_row % 2] + cw_from + ccw_from).astype(jnp.int32), cut, *inv)

    cut = to_column(turned.reshape(tiles, rows, share, slab))
    ring = ring_of(cols)
    ahead = [(ring[i], ring[(i + 1) % cols]) for i in range(cols)]
    back = [(b, a) for a, b in ahead]
    part = slab // 2
    mine = lax.dynamic_slice_in_dim(inverse, (my_row % 2) * part, part, 0)
    left = pan_left
    inv_cw, inv_ccw = [mine[: part // 2]], [mine[part // 2 :]]
    last = cols - 1
    marks = [max(1, round(last * m / 7)) for m in range(8)]
    split = split_steps(cols, half)
    cw, ccw = [turned[:half]], [turned[half:]]
    now = [[turned[part * half + k] for k in range(half)] for part in range(2)]
    for step in range(1, cols):
        held = [lax.ppermute(inv_cw[-1], "col", ahead), lax.ppermute(inv_ccw[-1], "col", back)]
        tile = (step - 1) % half
        going = step <= split * half
        if going:
            held += [lax.ppermute(now[0][tile], "col", ahead), lax.ppermute(now[1][tile], "col", back)]
        if step == marks[2]:
            held, cut, left = lax.optimization_barrier((held, cut, left))
            left = to_column(left.reshape(tiles, rows, piece, rank))
        elif step == marks[4]:
            held, cut, left = lax.optimization_barrier((held, cut, left))
            cut = lax.all_to_all(cut, "col", 0, 0, tiled=True)
        elif step == last:
            held, cut, left = lax.optimization_barrier((held, cut, left))
        else:
            held = lax.optimization_barrier(held)
        inv_cw.append(held[0])
        inv_ccw.append(held[1])
        if going:
            now[0][tile], now[1][tile] = held[2:]
            if tile == half - 1:
                cw.append(tuple(now[0]))
                ccw.append(tuple(now[1]))
    inv = [jnp.stack(inv_cw), jnp.stack(inv_ccw)]
    inv = inv + swap_cores(inv, rows)
    solved = solve(cut, inv)
    first = [gather_y(part, rows) for part in solved[: per // 2]]
    left = lax.all_to_all(left, "col", 0, 0, tiled=True)
    held = (jnp.stack(now[0]), jnp.stack(now[1]))
    marks = [max(1, round((last - split) * m / 4)) for m in range(5)]
    for step in range(1, last - split + 1):
        cw.append(lax.ppermute(held[0], "col", ahead))
        ccw.append(lax.ppermute(held[1], "col", back))
        held = (cw[-1], ccw[-1])
        if step == marks[1]:
            held, left, first = lax.optimization_barrier((held, left, first))
            second = [gather_y(part, rows) for part in solved[per // 2 :]]
            ours = [part + swap_cores(part, rows) for part in first]
        elif step == marks[2]:
            held, second, ours = lax.optimization_barrier((held, second, ours))
            left = [left[: cols // 2], left[cols // 2 :]]
            left[0] = gather_y(left[0], rows)
            ours = ours + [part + swap_cores(part, rows) for part in second]
        elif step == marks[3]:
            held, left[0], ours = lax.optimization_barrier((held, left[0], ours))
            left[1] = gather_y(left[1], rows)
            left[0] = left[0] + swap_cores(left[0], rows)
        elif step == last - split:
            held, left = lax.optimization_barrier((held, left))
            left[1] = left[1] + swap_cores(left[1], rows)
        else:
            held = lax.optimization_barrier(held)
        cw[-1], ccw[-1] = held
    my_ranks = lax.dynamic_slice_in_dim(rank_list, my_row * tiles, tiles, 0)
    their_ranks = lax.dynamic_slice_in_dim(rank_list, my_col * per, per, 0)
    meta = jnp.concatenate([jnp.stack(ids + cw_from + ccw_from).astype(jnp.int32), my_ranks, their_ranks])
    operands = [a for part in cw + ccw for a in (part if isinstance(part, tuple) else (part,))]
    operands += [a for group in ours + left for a in group]
    update, gram = pl.pallas_call(
        functools.partial(main_kernel, cols, rows, tiles, per),
        out_shape=(
            jax.ShapeDtypeStruct((tiles, per, size, rank), jnp.bfloat16),
            jax.ShapeDtypeStruct((tiles, per, rank, rank), jnp.bfloat16),
        ),
        in_specs=[smem] + [anywhere] * len(operands),
        out_specs=(anywhere, anywhere),
        scratch_shapes=[
            pltpu.VMEM((tiles, rank, size), jnp.bfloat16),
            pltpu.VMEM((per, rank, size), jnp.bfloat16),
            pltpu.VMEM((per, cols, rows, piece, rank), jnp.bfloat16),
            pltpu.VMEM((2, size, rank), jnp.bfloat16),
            pltpu.VMEM((2, rank, rank), jnp.bfloat16),
            pltpu.SemaphoreType.DMA((tiles, cols)),
            pltpu.SemaphoreType.DMA((per, rows)),
            pltpu.SemaphoreType.DMA((2, rows, per)),
            pltpu.SemaphoreType.DMA((2, 2)),
        ],
        compiler_params=pltpu.CompilerParams(vmem_limit_bytes=60 * MIB),
        cost_estimate=pl.CostEstimate(
            flops=tiles * per * (6 * rank * rank * size),
            bytes_accessed=2 * tiles * per * size * rank + 2 * size * rank * (tiles + 2 * per),
            transcendentals=0,
        ),
        name="main",
    )(meta, *operands)
    return update, gram


def solution(mesh):
    in_specs = (P("row", "col", None), P("row", "col", None), P("col", None), P())
    out_specs = (P("row", "col", None, None), P("row", "col", None, None))
    return jax.shard_map(local, mesh=mesh, in_specs=in_specs, out_specs=out_specs, check_vma=False)
```

```python
import functools

import jax
import jax.numpy as jnp
from jax import lax
from jax.experimental import pallas as pl
from jax.experimental.pallas import tpu as pltpu
from jax.sharding import PartitionSpec as P

NT = (((1,), (1,)), ((), ()))
NN = (((1,), (0,)), ((), ()))
TN = (((0,), (0,)), ((), ()))
BLOCK = 256
MIB = 1 << 20


def dot(a, b, dims):
    return lax.dot_general(a, b, dims, preferred_element_type=jnp.float32)


def ring_of(count):
    return list(range(0, count, 2)) + list(range(count - 1, 0, -2))


def ring_place(col, count):
    return jnp.where(col % 2 == 0, col // 2, count // 2 + (count - 1 - col) // 2)


def ring_col(place, count):
    place = place % count
    return jnp.where(place < count // 2, 2 * place, count - 1 - 2 * (place - count // 2))


def split_steps(cols, half):
    return (cols - 2) // half


def tie(array, *after):
    return lax.optimization_barrier((array, *after))[0]


def gather_y(piece, rows):
    return [piece] + [
        lax.ppermute(piece, "row", [(i, (i + 2 * step) % rows) for i in range(rows)]) for step in range(1, rows // 2)
    ]


def swap_cores(held, rows):
    return [lax.ppermute(h, "row", [(i, i ^ 1) for i in range(rows)]) for h in held]


def gather_row(piece, rows):
    held = gather_y(piece, rows)
    return held + swap_cores(held, rows)


def row_ids(my_row, rows):
    other = jnp.bitwise_xor(my_row, 1)
    half = rows // 2
    return [(my_row - 2 * k) % rows for k in range(half)] + [(other - 2 * k) % rows for k in range(half)]


def solve_kernel(cols, meta, cut, *refs):
    it = iter(refs)
    inv = [next(it) for _ in range(4)]
    per, share, width = cut.shape[1:]
    out = [next(it) for _ in range(per)]
    right, whole, solved, rsem, isem = it
    core = meta[0]
    pulls = []
    for s in range(cols):
        for j in range(per):
            target = right.at[pl.ds(j * share, share), pl.ds(s * width, width)]
            pulls.append(pltpu.make_async_copy(cut.at[s, j], target, rsem.at[s, j]))
        for k in range(2):
            source = meta[1 + k * cols + s]
            pulls.append(pltpu.make_async_copy(inv[k].at[s], whole.at[source, core, k], isem.at[s, k, 0]))
            pulls.append(pltpu.make_async_copy(inv[2 + k].at[s], whole.at[source, 1 - core, k], isem.at[s, k, 1]))
    for copy in pulls:
        copy.start()
    for copy in pulls:
        copy.wait()
    size = right.shape[1]
    flat = whole.reshape(size, size)
    for b in range(size // BLOCK):
        end = (b + 1) * BLOCK
        solved[:, b * BLOCK : end] = dot(right[:, :end], flat[b * BLOCK : end, :end], NT).astype(jnp.bfloat16)
    for b in range(size // BLOCK):
        start = b * BLOCK
        value = dot(solved[:, start:], flat[start:, start : start + BLOCK], NN).astype(jnp.bfloat16)
        for j in range(per):
            out[j][:, start : start + BLOCK] = value[j * share : (j + 1) * share]


def messages(it, cols, tiles, steps):
    half, split, found = tiles // 2, split_steps(cols, tiles // 2), []
    for step in steps:
        if 1 <= step <= split:
            found.append([next(it) for _ in range(half)])
        else:
            whole = next(it)
            found.append([whole.at[k] for k in range(half)])
    return found


def core_kernel(cols, rows, tiles, per, meta, *refs):
    it = iter(refs)
    early = cols - 1
    came = [messages(it, cols, tiles, range(early)) for _ in range(2)]
    ours = [[next(it) for _ in range(rows)] for _ in range(per)]
    total, right, turned, value, rsem, tsem, osem = it
    half = tiles // 2
    size, width, rank = right.shape[2], right.shape[2] // cols, right.shape[1]
    share, cut = ours[0][0].shape[0], rank // 2
    base = rows + 2 * cols

    def turned_copies():
        spots = [pl.multiple_of(meta[k] * share, share) for k in range(rows)]
        return [
            pltpu.make_async_copy(ours[j][k], turned.at[j, pl.ds(spots[k], share), :], tsem.at[j, k])
            for j in range(per)
            for k in range(rows)
        ]

    def spots_of(part):
        return [pl.multiple_of(meta[rows + part * cols + s] * width, width) for s in range(cols)]

    def right_copies(tile):
        spots = spots_of(tile // half)
        return [
            pltpu.make_async_copy(
                came[tile // half][s][tile % half], right.at[tile, :, pl.ds(spots[s], width)], rsem.at[tile, s]
            )
            for s in range(early)
        ]

    for copy in turned_copies():
        copy.start()
    for tile in range(tiles):
        for copy in right_copies(tile):
            copy.start()
        right[tile, :, pl.ds(spots_of(tile // half)[early], width)] = jnp.zeros((rank, width), jnp.bfloat16)
    for copy in turned_copies():
        copy.wait()

    def out(i, j, slot):
        return pltpu.make_async_copy(value.at[slot], total.at[i, j], osem.at[slot])

    def pair(at, carry):
        i, j, slot = at // per, at % per, at % 2
        for tile in range(tiles):

            @pl.when(at == tile * per)
            def _(tile=tile):
                for copy in right_copies(tile):
                    copy.wait()

        @pl.when(at >= 2)
        def _():
            out(i, j, slot).wait()

        for tall in (cut, rank):
            for wide in (cut, rank):
                low = meta[base + i] <= cut if tall == cut else meta[base + i] > cut
                thin = meta[base + tiles + j] <= cut if wide == cut else meta[base + tiles + j] > cut

                @pl.when(jnp.logical_and(low, thin))
                def _(tall=tall, wide=wide):
                    value[slot, :tall, :wide] = dot(right[i, :tall], turned[j, :wide], NT)

        out(i, j, slot).start()
        return carry

    count = tiles * per
    lax.fori_loop(0, count, pair, 0)
    for at in range(max(0, count - 2), count):
        out(at // per, at % per, at % 2).wait()


def main_kernel(cols, rows, tiles, per, meta, *refs):
    it = iter(refs)
    came = [messages(it, cols, tiles, [cols - 1])[0] for _ in range(2)]
    ours = [[next(it) for _ in range(rows)] for _ in range(per)]
    left = [[next(it) for _ in range(rows)] for _ in range(2)]
    early = next(it)
    update, gram = next(it), next(it)
    right, turned, whole, sums, upd, grm, rsem, tsem, lsem, ssem, osem = it
    half = tiles // 2
    width, rank = right.shape[2], right.shape[1]
    size = width * cols
    share, some = ours[0][0].shape[0], left[0][0].shape[0]
    base = rows + 2 * cols

    def small_copies():
        rank_spots = [pl.multiple_of(meta[k] * share, share) for k in range(rows)]
        copies = [
            pltpu.make_async_copy(came[tile // half][tile % half], right.at[tile], rsem.at[tile])
            for tile in range(tiles)
        ]
        for part in range(2):
            spot = pl.multiple_of(meta[rows + part * cols + cols - 1] * width, width)
            for j in range(per):
                for k in range(rows):
                    copies.append(
                        pltpu.make_async_copy(
                            ours[j][k].at[:, pl.ds(spot, width)],
                            turned.at[part, j, pl.ds(rank_spots[k], share), :],
                            tsem.at[part, j, k],
                        )
                    )
        return copies

    def left_copies():
        return [
            pltpu.make_async_copy(
                left[h][k].at[:, j], whole.at[j, h * some : (h + 1) * some, meta[k]], lsem.at[h, k, j]
            )
            for j in range(per)
            for h in range(2)
            for k in range(rows)
        ]

    def sum_copy(at):
        return pltpu.make_async_copy(early.at[at // per, at % per], sums.at[at % 2], ssem.at[at % 2])

    for copy in small_copies():
        copy.start()
    sum_copy(0).start()
    for copy in left_copies():
        copy.start()
    for copy in small_copies():
        copy.wait()
    flat = whole.reshape(per, size, rank)
    row_at = lax.broadcasted_iota(jnp.int32, (rank, rank), 0)
    col_at = lax.broadcasted_iota(jnp.int32, (rank, rank), 1)
    cut = rank // 2

    def outs(i, j, slot):
        return (
            pltpu.make_async_copy(upd.at[slot], update.at[i, j], osem.at[0, slot]),
            pltpu.make_async_copy(grm.at[slot], gram.at[i, j], osem.at[1, slot]),
        )

    def pair(at, carry):
        i, j, slot = at // per, at % per, at % 2

        @pl.when(at + 1 < tiles * per)
        def _():
            sum_copy(at + 1).start()

        sum_copy(at).wait()

        @pl.when(at == 0)
        def _():
            for copy in left_copies():
                copy.wait()

        @pl.when(at >= 2)
        def _():
            for copy in outs(i, j, slot):
                copy.wait()

        def work(tall, wide):
            value = sums[slot, :tall, :wide] + dot(right[i, :tall], turned[i // half, j, :wide], NT)
            live = (row_at[:tall, :wide] < meta[base + i]) & (col_at[:tall, :wide] < meta[base + tiles + j])
            value = jnp.where(live, value, 0.0).astype(jnp.bfloat16)
            upd[slot, :, :tall] = dot(flat[j, :, :wide], value, NT).astype(jnp.bfloat16)
            if tall < rank:
                upd[slot, :, tall:] = jnp.zeros((size, rank - tall), jnp.bfloat16)
            outs(i, j, slot)[0].start()
            top = (dot(upd[slot, :, :cut], upd[slot, :, :tall], TN) / size).astype(jnp.bfloat16)
            grm[slot, :cut, :tall] = top
            if tall < rank:
                grm[slot, :cut, cut:] = jnp.zeros((cut, rank - cut), jnp.bfloat16)
                grm[slot, cut:] = jnp.zeros((rank - cut, rank), jnp.bfloat16)
            else:
                grm[slot, cut:, :cut] = top[:, cut:].T
                grm[slot, cut:, cut:] = (dot(upd[slot, :, cut:], upd[slot, :, cut:], TN) / size).astype(jnp.bfloat16)

        for tall in (cut, rank):
            for wide in (cut, rank):
                low = meta[base + i] <= cut if tall == cut else meta[base + i] > cut
                thin = meta[base + tiles + j] <= cut if wide == cut else meta[base + tiles + j] > cut

                @pl.when(jnp.logical_and(low, thin))
                def _(tall=tall, wide=wide):
                    work(tall, wide)

        outs(i, j, slot)[1].start()
        return carry

    total = tiles * per
    lax.fori_loop(0, total, pair, 0)
    for at in range(max(0, total - 2), total):
        for copy in outs(at // per, at % per, at % 2):
            copy.wait()


def to_column(pieces):
    moved = lax.all_to_all(pieces, "row", 1, 0, tiled=False)
    cols = lax.axis_size("col")
    moved = moved.reshape((cols, -1) + pieces.shape[2:])
    return moved


def local(pan_left, pan_right, inverse, rank_list):
    tiles, slab, rank = pan_right.shape
    size = inverse.shape[1]
    rows, cols = lax.axis_size("row"), lax.axis_size("col")
    per = tiles * rows // cols
    my_row, my_col = lax.axis_index("row"), lax.axis_index("col")
    piece = slab // rows
    share = rank // rows
    half = tiles // 2
    turned = jnp.swapaxes(pan_right, 1, 2)
    place = ring_place(my_col, cols)
    cw_from = [ring_col(place - s + cols, cols) for s in range(cols)]
    ccw_from = [ring_col(place + s, cols) for s in range(cols)]
    ids = row_ids(my_row, rows)
    anywhere = pl.BlockSpec(memory_space=pltpu.HBM)
    vmem = pl.BlockSpec(memory_space=pltpu.VMEM)
    smem = pl.BlockSpec(memory_space=pltpu.SMEM)

    def solve(cut, inv):
        return pl.pallas_call(
            functools.partial(solve_kernel, cols),
            out_shape=[jax.ShapeDtypeStruct((share, size), jnp.bfloat16)] * per,
            in_specs=[smem] + [anywhere] * 5,
            out_specs=[vmem] * per,
            scratch_shapes=[
                pltpu.VMEM((per * share, size), jnp.bfloat16),
                pltpu.VMEM((cols, 2, 2, slab // 4, size), jnp.bfloat16),
                pltpu.VMEM((per * share, size), jnp.bfloat16),
                pltpu.SemaphoreType.DMA((cols, per)),
                pltpu.SemaphoreType.DMA((cols, 2, 2)),
            ],
            compiler_params=pltpu.CompilerParams(vmem_limit_bytes=60 * MIB),
            cost_estimate=pl.CostEstimate(
                flops=2 * per * share * size * size, bytes_accessed=2 * size * (size + 2 * per * share), transcendentals=0
            ),
            name="solve",
        )(jnp.stack([my_row % 2] + cw_from + ccw_from).astype(jnp.int32), cut, *inv)

    my_ranks = lax.dynamic_slice_in_dim(rank_list, my_row * tiles, tiles, 0)
    their_ranks = lax.dynamic_slice_in_dim(rank_list, my_col * per, per, 0)
    meta = jnp.concatenate([jnp.stack(ids + cw_from + ccw_from).astype(jnp.int32), my_ranks, their_ranks])

    def core_sums(cw, ccw, ours):
        operands = [a for part in cw + ccw for a in (part if isinstance(part, tuple) else (part,))]
        operands += [a for group in ours for a in group]
        return pl.pallas_call(
            functools.partial(core_kernel, cols, rows, tiles, per),
            out_shape=jax.ShapeDtypeStruct((tiles, per, rank, rank), jnp.float32),
            in_specs=[smem] + [anywhere] * len(operands),
            out_specs=anywhere,
            scratch_shapes=[
                pltpu.VMEM((tiles, rank, size), jnp.bfloat16),
                pltpu.VMEM((per, rank, size), jnp.bfloat16),
                pltpu.VMEM((2, rank, rank), jnp.float32),
                pltpu.SemaphoreType.DMA((tiles, cols)),
                pltpu.SemaphoreType.DMA((per, rows)),
                pltpu.SemaphoreType.DMA((2,)),
            ],
            compiler_params=pltpu.CompilerParams(vmem_limit_bytes=60 * MIB),
            cost_estimate=pl.CostEstimate(
                flops=tiles * per * 2 * rank * rank * size,
                bytes_accessed=2 * size * rank * (tiles + per) + 4 * tiles * per * rank * rank,
                transcendentals=0,
            ),
            name="core",
        )(meta, *operands)

    cut = to_column(turned.reshape(tiles, rows, share, slab))
    ring = ring_of(cols)
    ahead = [(ring[i], ring[(i + 1) % cols]) for i in range(cols)]
    back = [(b, a) for a, b in ahead]
    part = slab // 2
    mine = lax.dynamic_slice_in_dim(inverse, (my_row % 2) * part, part, 0)
    left = pan_left
    inv_cw, inv_ccw = [mine[: part // 2]], [mine[part // 2 :]]
    last = cols - 1
    marks = [max(1, round(last * m / 7)) for m in range(8)]
    split = split_steps(cols, half)
    cw, ccw = [turned[:half]], [turned[half:]]
    now = [[turned[part * half + k] for k in range(half)] for part in range(2)]
    for step in range(1, cols):
        held = [lax.ppermute(inv_cw[-1], "col", ahead), lax.ppermute(inv_ccw[-1], "col", back)]
        tile = (step - 1) % half
        going = step <= split * half
        if going:
            held += [lax.ppermute(now[0][tile], "col", ahead), lax.ppermute(now[1][tile], "col", back)]
        if step == marks[2]:
            held, cut, left = lax.optimization_barrier((held, cut, left))
            left = to_column(left.reshape(tiles, rows, piece, rank))
        elif step == marks[4]:
            held, cut, left = lax.optimization_barrier((held, cut, left))
            cut = lax.all_to_all(cut, "col", 0, 0, tiled=True)
        elif step == last:
            held, cut, left = lax.optimization_barrier((held, cut, left))
        else:
            held = lax.optimization_barrier(held)
        inv_cw.append(held[0])
        inv_ccw.append(held[1])
        if going:
            now[0][tile], now[1][tile] = held[2:]
            if tile == half - 1:
                cw.append(tuple(now[0]))
                ccw.append(tuple(now[1]))
    inv = [jnp.stack(inv_cw), jnp.stack(inv_ccw)]
    inv = inv + swap_cores(inv, rows)
    solved = solve(cut, inv)
    first = [gather_y(part, rows) for part in solved[: per // 2]]
    left = lax.all_to_all(left, "col", 0, 0, tiled=True)
    held = (jnp.stack(now[0]), jnp.stack(now[1]))
    marks = [max(1, round((last - split) * m / 4)) for m in range(5)]
    for step in range(1, last - split + 1):
        cw.append(lax.ppermute(held[0], "col", ahead))
        ccw.append(lax.ppermute(held[1], "col", back))
        held = (cw[-1], ccw[-1])
        if step == marks[1]:
            held, left, first = lax.optimization_barrier((held, left, first))
            second = [gather_y(part, rows) for part in solved[per // 2 :]]
            ours = [part + swap_cores(part, rows) for part in first]
        elif step == marks[2]:
            held, second, ours = lax.optimization_barrier((held, second, ours))
            left = [left[: cols // 2], left[cols // 2 :]]
            left[0] = gather_y(left[0], rows)
            ours = ours + [part + swap_cores(part, rows) for part in second]
        elif step == marks[3]:
            held, left[0], ours = lax.optimization_barrier((held, left[0], ours))
            left[1] = gather_y(left[1], rows)
            left[0] = left[0] + swap_cores(left[0], rows)
        elif step == last - split:
            held, left, total = lax.optimization_barrier((held, left, total))
            left[1] = left[1] + swap_cores(left[1], rows)
        else:
            held = lax.optimization_barrier(held)
        cw[-1], ccw[-1] = held
        if step == last - split - 1:
            total = core_sums(cw, ccw, ours)
    operands = [cw[-1], ccw[-1]] + [a for group in ours + left for a in group] + [total]
    update, gram = pl.pallas_call(
        functools.partial(main_kernel, cols, rows, tiles, per),
        out_shape=(
            jax.ShapeDtypeStruct((tiles, per, size, rank), jnp.bfloat16),
            jax.ShapeDtypeStruct((tiles, per, rank, rank), jnp.bfloat16),
        ),
        in_specs=[smem] + [anywhere] * len(operands),
        out_specs=(anywhere, anywhere),
        scratch_shapes=[
            pltpu.VMEM((tiles, rank, slab), jnp.bfloat16),
            pltpu.VMEM((2, per, rank, slab), jnp.bfloat16),
            pltpu.VMEM((per, cols, rows, piece, rank), jnp.bfloat16),
            pltpu.VMEM((2, rank, rank), jnp.float32),
            pltpu.VMEM((2, size, rank), jnp.bfloat16),
            pltpu.VMEM((2, rank, rank), jnp.bfloat16),
            pltpu.SemaphoreType.DMA((tiles,)),
            pltpu.SemaphoreType.DMA((2, per, rows)),
            pltpu.SemaphoreType.DMA((2, rows, per)),
            pltpu.SemaphoreType.DMA((2,)),
            pltpu.SemaphoreType.DMA((2, 2)),
        ],
        compiler_params=pltpu.CompilerParams(vmem_limit_bytes=60 * MIB),
        cost_estimate=pl.CostEstimate(
            flops=tiles * per * (4 * rank * rank * size),
            bytes_accessed=2 * tiles * per * size * rank + 2 * size * rank * (tiles + 2 * per),
            transcendentals=0,
        ),
        name="main",
    )(meta, *operands)
    return update, gram


def solution(mesh):
    in_specs = (P("row", "col", None), P("row", "col", None), P("col", None), P())
    out_specs = (P("row", "col", None, None), P("row", "col", None, None))
    return jax.shard_map(local, mesh=mesh, in_specs=in_specs, out_specs=out_specs, check_vma=False)
```

```python
import functools

import jax
import jax.numpy as jnp
from jax import lax
from jax.experimental import pallas as pl
from jax.experimental.pallas import tpu as pltpu
from jax.sharding import PartitionSpec as P

NT = (((1,), (1,)), ((), ()))
NN = (((1,), (0,)), ((), ()))
TN = (((0,), (0,)), ((), ()))
BLOCK = 256
MIB = 1 << 20


def dot(a, b, dims):
    return lax.dot_general(a, b, dims, preferred_element_type=jnp.float32)


def ring_of(count):
    return list(range(0, count, 2)) + list(range(count - 1, 0, -2))


def ring_place(col, count):
    return jnp.where(col % 2 == 0, col // 2, count // 2 + (count - 1 - col) // 2)


def ring_col(place, count):
    place = place % count
    return jnp.where(place < count // 2, 2 * place, count - 1 - 2 * (place - count // 2))


def split_steps(cols, half):
    return -(-(cols - 1) // half)


def tie(array, *after):
    return lax.optimization_barrier((array, *after))[0]


def gather_y(piece, rows):
    return [piece] + [
        lax.ppermute(piece, "row", [(i, (i + 2 * step) % rows) for i in range(rows)]) for step in range(1, rows // 2)
    ]


def swap_cores(held, rows):
    return [lax.ppermute(h, "row", [(i, i ^ 1) for i in range(rows)]) for h in held]


def gather_row(piece, rows):
    held = gather_y(piece, rows)
    return held + swap_cores(held, rows)


def row_ids(my_row, rows):
    other = jnp.bitwise_xor(my_row, 1)
    half = rows // 2
    return [(my_row - 2 * k) % rows for k in range(half)] + [(other - 2 * k) % rows for k in range(half)]


def solve_kernel(cols, meta, cut, *refs):
    it = iter(refs)
    inv = [next(it) for _ in range(4)]
    per, share, width = cut.shape[1:]
    out = [next(it) for _ in range(per)]
    right, whole, solved, rsem, isem = it
    core = meta[0]
    pulls = []
    for s in range(cols):
        for j in range(per):
            target = right.at[pl.ds(j * share, share), pl.ds(s * width, width)]
            pulls.append(pltpu.make_async_copy(cut.at[s, j], target, rsem.at[s, j]))
        for k in range(2):
            source = meta[1 + k * cols + s]
            pulls.append(pltpu.make_async_copy(inv[k].at[s], whole.at[source, core, k], isem.at[s, k, 0]))
            pulls.append(pltpu.make_async_copy(inv[2 + k].at[s], whole.at[source, 1 - core, k], isem.at[s, k, 1]))
    for copy in pulls:
        copy.start()
    for copy in pulls:
        copy.wait()
    size = right.shape[1]
    flat = whole.reshape(size, size)
    for b in range(size // BLOCK):
        end = (b + 1) * BLOCK
        solved[:, b * BLOCK : end] = dot(right[:, :end], flat[b * BLOCK : end, :end], NT).astype(jnp.bfloat16)
    for b in range(size // BLOCK):
        start = b * BLOCK
        value = dot(solved[:, start:], flat[start:, start : start + BLOCK], NN).astype(jnp.bfloat16)
        for j in range(per):
            out[j][:, start : start + BLOCK] = value[j * share : (j + 1) * share]


def messages(it, cols, tiles, steps):
    half, split, found = tiles // 2, split_steps(cols, tiles // 2), []
    for step in steps:
        if 1 <= step <= split:
            found.append([next(it) for _ in range(half)])
        else:
            whole = next(it)
            found.append([whole.at[k] for k in range(half)])
    return found


def core_kernel(cols, rows, tiles, per, meta, *refs):
    it = iter(refs)
    early = cols - 1
    came = [messages(it, cols, tiles, range(early)) for _ in range(2)]
    ours = [[next(it) for _ in range(rows)] for _ in range(per)]
    total, right, turned, value, rsem, tsem, osem = it
    half = tiles // 2
    size, width, rank = right.shape[2], right.shape[2] // cols, right.shape[1]
    share, cut = ours[0][0].shape[0], rank // 2
    base = rows + 2 * cols

    def turned_copies():
        spots = [pl.multiple_of(meta[k] * share, share) for k in range(rows)]
        return [
            pltpu.make_async_copy(ours[j][k], turned.at[j, pl.ds(spots[k], share), :], tsem.at[j, k])
            for j in range(per)
            for k in range(rows)
        ]

    def spots_of(part):
        return [pl.multiple_of(meta[rows + part * cols + s] * width, width) for s in range(cols)]

    def right_copies(tile):
        spots = spots_of(tile // half)
        return [
            pltpu.make_async_copy(
                came[tile // half][s][tile % half], right.at[tile, :, pl.ds(spots[s], width)], rsem.at[tile, s]
            )
            for s in range(early)
        ]

    for copy in turned_copies():
        copy.start()
    for tile in range(tiles):
        for copy in right_copies(tile):
            copy.start()
        right[tile, :, pl.ds(spots_of(tile // half)[early], width)] = jnp.zeros((rank, width), jnp.bfloat16)
    for copy in turned_copies():
        copy.wait()

    def out(i, j, slot):
        return pltpu.make_async_copy(value.at[slot], total.at[i, j], osem.at[slot])

    def pair(at, carry):
        i, j, slot = at // per, at % per, at % 2
        for tile in range(tiles):

            @pl.when(at == tile * per)
            def _(tile=tile):
                for copy in right_copies(tile):
                    copy.wait()

        @pl.when(at >= 2)
        def _():
            out(i, j, slot).wait()

        for tall in (cut, rank):
            for wide in (cut, rank):
                low = meta[base + i] <= cut if tall == cut else meta[base + i] > cut
                thin = meta[base + tiles + j] <= cut if wide == cut else meta[base + tiles + j] > cut

                @pl.when(jnp.logical_and(low, thin))
                def _(tall=tall, wide=wide):
                    value[slot, :tall, :wide] = dot(right[i, :tall], turned[j, :wide], NT)

        out(i, j, slot).start()
        return carry

    count = tiles * per
    lax.fori_loop(0, count, pair, 0)
    for at in range(max(0, count - 2), count):
        out(at // per, at % per, at % 2).wait()


def main_kernel(cols, rows, tiles, per, meta, *refs):
    it = iter(refs)
    came = [messages(it, cols, tiles, [cols - 1])[0] for _ in range(2)]
    ours = [[next(it) for _ in range(rows)] for _ in range(per)]
    left = [[next(it) for _ in range(rows)] for _ in range(2)]
    early = next(it)
    update, gram = next(it), next(it)
    right, turned, whole, sums, upd, grm, rsem, tsem, lsem, ssem, osem = it
    half = tiles // 2
    width, rank = right.shape[2], right.shape[1]
    size = width * cols
    share, some = ours[0][0].shape[0], left[0][0].shape[0]
    base = rows + 2 * cols

    def small_copies():
        rank_spots = [pl.multiple_of(meta[k] * share, share) for k in range(rows)]
        copies = [
            pltpu.make_async_copy(came[tile // half][tile % half], right.at[tile], rsem.at[tile])
            for tile in range(tiles)
        ]
        for part in range(2):
            spot = pl.multiple_of(meta[rows + part * cols + cols - 1] * width, width)
            for j in range(per):
                for k in range(rows):
                    copies.append(
                        pltpu.make_async_copy(
                            ours[j][k].at[:, pl.ds(spot, width)],
                            turned.at[part, j, pl.ds(rank_spots[k], share), :],
                            tsem.at[part, j, k],
                        )
                    )
        return copies

    def left_copies():
        return [
            pltpu.make_async_copy(
                left[h][k].at[:, j], whole.at[j, h * some : (h + 1) * some, meta[k]], lsem.at[h, k, j]
            )
            for j in range(per)
            for h in range(2)
            for k in range(rows)
        ]

    def sum_copy(at):
        return pltpu.make_async_copy(early.at[at // per, at % per], sums.at[at % 2], ssem.at[at % 2])

    for copy in small_copies():
        copy.start()
    sum_copy(0).start()
    for copy in left_copies():
        copy.start()
    for copy in small_copies():
        copy.wait()
    flat = whole.reshape(per, size, rank)
    row_at = lax.broadcasted_iota(jnp.int32, (rank, rank), 0)
    col_at = lax.broadcasted_iota(jnp.int32, (rank, rank), 1)
    cut = rank // 2

    def outs(i, j, slot):
        return (
            pltpu.make_async_copy(upd.at[slot], update.at[i, j], osem.at[0, slot]),
            pltpu.make_async_copy(grm.at[slot], gram.at[i, j], osem.at[1, slot]),
        )

    def pair(at, carry):
        i, j, slot = at // per, at % per, at % 2

        @pl.when(at + 1 < tiles * per)
        def _():
            sum_copy(at + 1).start()

        sum_copy(at).wait()

        @pl.when(at == 0)
        def _():
            for copy in left_copies():
                copy.wait()

        @pl.when(at >= 2)
        def _():
            for copy in outs(i, j, slot):
                copy.wait()

        def work(tall, wide):
            value = sums[slot, :tall, :wide] + dot(right[i, :tall], turned[i // half, j, :wide], NT)
            live = (row_at[:tall, :wide] < meta[base + i]) & (col_at[:tall, :wide] < meta[base + tiles + j])
            value = jnp.where(live, value, 0.0).astype(jnp.bfloat16)
            upd[slot, :, :tall] = dot(flat[j, :, :wide], value, NT).astype(jnp.bfloat16)
            if tall < rank:
                upd[slot, :, tall:] = jnp.zeros((size, rank - tall), jnp.bfloat16)
            outs(i, j, slot)[0].start()
            top = (dot(upd[slot, :, :cut], upd[slot, :, :tall], TN) / size).astype(jnp.bfloat16)
            grm[slot, :cut, :tall] = top
            if tall < rank:
                grm[slot, :cut, cut:] = jnp.zeros((cut, rank - cut), jnp.bfloat16)
                grm[slot, cut:] = jnp.zeros((rank - cut, rank), jnp.bfloat16)
            else:
                grm[slot, cut:, :cut] = top[:, cut:].T
                grm[slot, cut:, cut:] = (dot(upd[slot, :, cut:], upd[slot, :, cut:], TN) / size).astype(jnp.bfloat16)

        for tall in (cut, rank):
            for wide in (cut, rank):
                low = meta[base + i] <= cut if tall == cut else meta[base + i] > cut
                thin = meta[base + tiles + j] <= cut if wide == cut else meta[base + tiles + j] > cut

                @pl.when(jnp.logical_and(low, thin))
                def _(tall=tall, wide=wide):
                    work(tall, wide)

        outs(i, j, slot)[1].start()
        return carry

    total = tiles * per
    lax.fori_loop(0, total, pair, 0)
    for at in range(max(0, total - 2), total):
        for copy in outs(at // per, at % per, at % 2):
            copy.wait()


def to_column(pieces):
    moved = lax.all_to_all(pieces, "row", 1, 0, tiled=False)
    cols = lax.axis_size("col")
    moved = moved.reshape((cols, -1) + pieces.shape[2:])
    return moved


def local(pan_left, pan_right, inverse, rank_list):
    tiles, slab, rank = pan_right.shape
    size = inverse.shape[1]
    rows, cols = lax.axis_size("row"), lax.axis_size("col")
    per = tiles * rows // cols
    my_row, my_col = lax.axis_index("row"), lax.axis_index("col")
    piece = slab // rows
    share = rank // rows
    half = tiles // 2
    turned = jnp.swapaxes(pan_right, 1, 2)
    place = ring_place(my_col, cols)
    cw_from = [ring_col(place - s + cols, cols) for s in range(cols)]
    ccw_from = [ring_col(place + s, cols) for s in range(cols)]
    ids = row_ids(my_row, rows)
    anywhere = pl.BlockSpec(memory_space=pltpu.HBM)
    vmem = pl.BlockSpec(memory_space=pltpu.VMEM)
    smem = pl.BlockSpec(memory_space=pltpu.SMEM)

    def solve(cut, inv):
        return pl.pallas_call(
            functools.partial(solve_kernel, cols),
            out_shape=[jax.ShapeDtypeStruct((share, size), jnp.bfloat16)] * per,
            in_specs=[smem] + [anywhere] * 5,
            out_specs=[vmem] * per,
            scratch_shapes=[
                pltpu.VMEM((per * share, size), jnp.bfloat16),
                pltpu.VMEM((cols, 2, 2, slab // 4, size), jnp.bfloat16),
                pltpu.VMEM((per * share, size), jnp.bfloat16),
                pltpu.SemaphoreType.DMA((cols, per)),
                pltpu.SemaphoreType.DMA((cols, 2, 2)),
            ],
            compiler_params=pltpu.CompilerParams(vmem_limit_bytes=60 * MIB),
            cost_estimate=pl.CostEstimate(
                flops=2 * per * share * size * size, bytes_accessed=2 * size * (size + 2 * per * share), transcendentals=0
            ),
            name="solve",
        )(jnp.stack([my_row % 2] + cw_from + ccw_from).astype(jnp.int32), cut, *inv)

    my_ranks = lax.dynamic_slice_in_dim(rank_list, my_row * tiles, tiles, 0)
    their_ranks = lax.dynamic_slice_in_dim(rank_list, my_col * per, per, 0)
    meta = jnp.concatenate([jnp.stack(ids + cw_from + ccw_from).astype(jnp.int32), my_ranks, their_ranks])

    def core_sums(cw, ccw, ours):
        operands = [a for part in cw + ccw for a in (part if isinstance(part, tuple) else (part,))]
        operands += [a for group in ours for a in group]
        return pl.pallas_call(
            functools.partial(core_kernel, cols, rows, tiles, per),
            out_shape=jax.ShapeDtypeStruct((tiles, per, rank, rank), jnp.float32),
            in_specs=[smem] + [anywhere] * len(operands),
            out_specs=anywhere,
            scratch_shapes=[
                pltpu.VMEM((tiles, rank, size), jnp.bfloat16),
                pltpu.VMEM((per, rank, size), jnp.bfloat16),
                pltpu.VMEM((2, rank, rank), jnp.float32),
                pltpu.SemaphoreType.DMA((tiles, cols)),
                pltpu.SemaphoreType.DMA((per, rows)),
                pltpu.SemaphoreType.DMA((2,)),
            ],
            compiler_params=pltpu.CompilerParams(vmem_limit_bytes=60 * MIB),
            cost_estimate=pl.CostEstimate(
                flops=tiles * per * 2 * rank * rank * size,
                bytes_accessed=2 * size * rank * (tiles + per) + 4 * tiles * per * rank * rank,
                transcendentals=0,
            ),
            name="core",
        )(meta, *operands)

    cut = to_column(turned.reshape(tiles, rows, share, slab))
    ring = ring_of(cols)
    ahead = [(ring[i], ring[(i + 1) % cols]) for i in range(cols)]
    back = [(b, a) for a, b in ahead]
    part = slab // 2
    mine = lax.dynamic_slice_in_dim(inverse, (my_row % 2) * part, part, 0)
    left = pan_left
    inv_cw, inv_ccw = [mine[: part // 2]], [mine[part // 2 :]]
    last = cols - 1
    marks = [max(1, round(last * m / 7)) for m in range(8)]
    split = split_steps(cols, half)
    cw, ccw = [turned[:half]], [turned[half:]]
    now = [[turned[part * half + k] for k in range(half)] for part in range(2)]
    for step in range(1, cols):
        held = [lax.ppermute(inv_cw[-1], "col", ahead), lax.ppermute(inv_ccw[-1], "col", back)]
        tile = (step - 1) % half
        held += [lax.ppermute(now[0][tile], "col", ahead), lax.ppermute(now[1][tile], "col", back)]
        if step == marks[2]:
            held, cut, left = lax.optimization_barrier((held, cut, left))
            left = to_column(left.reshape(tiles, rows, piece, rank))
        elif step == marks[4]:
            held, cut, left = lax.optimization_barrier((held, cut, left))
            cut = lax.all_to_all(cut, "col", 0, 0, tiled=True)
        elif step == marks[6]:
            held, cut, left = lax.optimization_barrier((held, cut, left))
            left = lax.all_to_all(left, "col", 0, 0, tiled=True)
        else:
            held = lax.optimization_barrier(held)
        inv_cw.append(held[0])
        inv_ccw.append(held[1])
        now[0][tile], now[1][tile] = held[2:]
        if tile == half - 1:
            cw.append(tuple(now[0]))
            ccw.append(tuple(now[1]))
    inv = [jnp.stack(inv_cw), jnp.stack(inv_ccw)]
    inv = inv + swap_cores(inv, rows)
    solved = solve(cut, inv)
    first = [gather_y(part, rows) for part in solved[: per // 2]]
    if last % half:
        held = [[lax.ppermute(t, "col", way) for t in now[k][last % half :]] for k, way in enumerate((ahead, back))]
        held, left, first = lax.optimization_barrier((held, left, first))
        for k in range(2):
            now[k][last % half :] = held[k]
        cw.append(tuple(now[0]))
        ccw.append(tuple(now[1]))
    else:
        left, first = lax.optimization_barrier((left, first))
    second = [gather_y(part, rows) for part in solved[per // 2 :]]
    ours = [part + swap_cores(part, rows) for part in first]
    held = (jnp.stack(now[0]), jnp.stack(now[1]))
    marks = [max(1, round((last - split) * m / 3)) for m in range(4)]
    for step in range(1, last - split + 1):
        cw.append(lax.ppermute(held[0], "col", ahead))
        ccw.append(lax.ppermute(held[1], "col", back))
        held = (cw[-1], ccw[-1])
        if step == marks[1]:
            held, second, ours = lax.optimization_barrier((held, second, ours))
            left = [left[: cols // 2], left[cols // 2 :]]
            left[0] = gather_y(left[0], rows)
            ours = ours + [part + swap_cores(part, rows) for part in second]
        elif step == marks[2]:
            held, left[0], ours = lax.optimization_barrier((held, left[0], ours))
            left[1] = gather_y(left[1], rows)
            left[0] = left[0] + swap_cores(left[0], rows)
        elif step == last - split:
            held, left, total = lax.optimization_barrier((held, left, total))
            left[1] = left[1] + swap_cores(left[1], rows)
        else:
            held = lax.optimization_barrier(held)
        cw[-1], ccw[-1] = held
        if step == last - split - 1:
            total = core_sums(cw, ccw, ours)
    operands = [cw[-1], ccw[-1]] + [a for group in ours + left for a in group] + [total]
    update, gram = pl.pallas_call(
        functools.partial(main_kernel, cols, rows, tiles, per),
        out_shape=(
            jax.ShapeDtypeStruct((tiles, per, size, rank), jnp.bfloat16),
            jax.ShapeDtypeStruct((tiles, per, rank, rank), jnp.bfloat16),
        ),
        in_specs=[smem] + [anywhere] * len(operands),
        out_specs=(anywhere, anywhere),
        scratch_shapes=[
            pltpu.VMEM((tiles, rank, slab), jnp.bfloat16),
            pltpu.VMEM((2, per, rank, slab), jnp.bfloat16),
            pltpu.VMEM((per, cols, rows, piece, rank), jnp.bfloat16),
            pltpu.VMEM((2, rank, rank), jnp.float32),
            pltpu.VMEM((2, size, rank), jnp.bfloat16),
            pltpu.VMEM((2, rank, rank), jnp.bfloat16),
            pltpu.SemaphoreType.DMA((tiles,)),
            pltpu.SemaphoreType.DMA((2, per, rows)),
            pltpu.SemaphoreType.DMA((2, rows, per)),
            pltpu.SemaphoreType.DMA((2,)),
            pltpu.SemaphoreType.DMA((2, 2)),
        ],
        compiler_params=pltpu.CompilerParams(vmem_limit_bytes=60 * MIB),
        cost_estimate=pl.CostEstimate(
            flops=tiles * per * (4 * rank * rank * size),
            bytes_accessed=2 * tiles * per * size * rank + 2 * size * rank * (tiles + 2 * per),
            transcendentals=0,
        ),
        name="main",
    )(meta, *operands)
    return update, gram


def solution(mesh):
    in_specs = (P("row", "col", None), P("row", "col", None), P("col", None), P())
    out_specs = (P("row", "col", None, None), P("row", "col", None, None))
    return jax.shard_map(local, mesh=mesh, in_specs=in_specs, out_specs=out_specs, check_vma=False)
```
